32 devices in a mesh: grp: 2 (over x), ao: 16 (over z, y, core).
Axes of the slice: x: 2, y: 2, z: 4, core: 2. Of those that a mesh axis runs over, the one named last changes fastest.
Arguments:
- chol_tiles: bfloat16 [32, 64, 128, 128], P(('grp', 'ao')), parts along dimension 0, may hold values from -6 to 6
- orbitals: bfloat16 [8192, 440], P('grp'), parts along dimension 0, may hold values from -0.29882812 to 0.29882812
- rdm_two: bfloat16 [3200, 1600], P('grp'), parts along dimension 0, may hold values from -0.0014648438 to 0.0014648438
- tile_row: int32 [32], P('grp'), parts along dimension 0, may hold values from 0 to 31
- tile_col: int32 [32], P('grp'), parts along dimension 0, may hold values from 0 to 31
- tile_live: int32 [32], P('grp'), parts along dimension 0, may hold values 0 or 1
Outputs:
- b_vectors: bfloat16 [128, 40, 440], P(('grp', 'ao')), parts along dimension 0
- q_matrix: float32 [880, 40], P('grp'), parts along dimension 0
The draws below stay inside these ranges and needn't reach their ends.
There are 2 independent parts, one for each index of `grp`. The reference program is written for one: setup_inputs(seed, part) draws one part's arguments, and reference() takes and returns one part's arrays. A program takes and returns all parts, laid end to end along the dimension named above; each array names one. Nothing has to cross between parts.
All inputs are finite; a program needn't handle non-finite values.
Results may differ from the reference program's by a relative error of at most 0.0064.
Values may be sent and summed in bfloat16 or wider, within the bound.
A program may use at most 128 MiB of HBM per device.

```python
import jax
import jax.numpy as jnp
from jax import lax

TILE = 128
NAO = 4096
ACT = 40
NT = 32
NORB = 440
VEC = 64
SLOTS = 16


def set_ends(entries, stream_key, low, top_value):
    longest = entries.shape.index(max(entries.shape))
    spots = []
    for shift in (0, 1):
        where = [jax.random.randint(jax.random.fold_in(stream_key, axis), (), 0, length) for axis, length in enumerate(entries.shape)]
        where[longest] = (where[longest] + shift) % entries.shape[longest]
        spots.append(tuple(where))
    return entries.at[spots[0]].set(low).at[spots[1]].set(top_value)


def block_scale(own_key, dims, pieces, smallest, top_value):
    loudness, own = 1.0, jax.random.fold_in(own_key, 6)
    for position, shards_of in pieces:
        draws = jnp.exp(jax.random.uniform(jax.random.fold_in(own, position), (shards_of,), jnp.float32, smallest / len(pieces), top_value / len(pieces)))
        loudness = loudness * jnp.repeat(draws, dims[position] // shards_of).reshape([-1 if axis == position else 1 for axis in range(len(dims))])
    return loudness


def noise(own_key, shape, spread, most, cuts=(), kind=jnp.bfloat16):
    loudness = block_scale(own_key, shape, cuts, -0.22, 0.18) if cuts else 1.0
    array = jax.random.normal(own_key, shape, jnp.float32) * spread * loudness
    return jnp.minimum(jnp.maximum(array, -most), most).astype(kind)


def setup_inputs(seed: int = 0, part: int = 0) -> dict:
    key_list = jax.random.split(jax.random.key(seed), 7)
    part_splits = jax.random.split(jax.random.fold_in(key_list[6], part), 7)
    return {
        "chol_tiles": noise(part_splits[0], (SLOTS, VEC, TILE, TILE), 1.0, 6.0, ((0, 16),)),
        "orbitals": noise(part_splits[1], (NAO, NORB), 0.05, 0.29882812),
        "rdm_two": noise(part_splits[2], (ACT * ACT, ACT * ACT), (0.005 * (ACT * VEC) ** -0.5), 0.0014648438),
        "tile_row": set_ends(jax.random.randint(part_splits[3], (SLOTS,), 0, NT), jax.random.fold_in(part_splits[3], 1), 0, NT - 1).astype(jnp.int32),
        "tile_col": set_ends(jax.random.randint(part_splits[4], (SLOTS,), 0, NT), jax.random.fold_in(part_splits[4], 1), 0, NT - 1).astype(jnp.int32),
        "tile_live": set_ends((jax.random.randint(part_splits[5], (SLOTS,), 0, 4) < 3).astype(jnp.int32), jax.random.fold_in(part_splits[5], 1), 0, 1),
    }


def reference(chol_tiles, orbitals, rdm_two, tile_row, tile_col, tile_live):
    ntiles = NAO // TILE
    coef = orbitals.astype(jnp.float32).reshape(ntiles, TILE, NORB)
    rows_coef = coef[tile_row.astype(jnp.int32)]
    cols_coef = coef[tile_col.astype(jnp.int32)][:, :, :ACT]
    half = jnp.einsum('svmn,sna->vsam', chol_tiles.astype(jnp.float32), cols_coef)
    half = (half * tile_live.astype(jnp.float32)[None, :, None, None]).astype(jnp.bfloat16)
    b_vectors = jnp.einsum('vsam,smp->vap', half.astype(jnp.float32), rows_coef).astype(jnp.bfloat16)
    flat = b_vectors[:, :, :ACT].reshape(VEC, ACT * ACT)
    zeta = jnp.dot(flat, rdm_two, preferred_element_type=jnp.float32).reshape(VEC, ACT, ACT)
    q_matrix = jnp.einsum('vup,vtu->pt', b_vectors.astype(jnp.float32), zeta, precision=lax.Precision.HIGHEST)
    return b_vectors, q_matrix
```

```python
import jax
import jax.numpy as jnp
from jax import lax
from jax.sharding import PartitionSpec as P

TILE = 128
ACT = 40


def on_device(chol_tiles, orbitals, rdm_two, tile_row, tile_col, tile_live):
    nao = orbitals.shape[0]
    norb = orbitals.shape[1]
    ntiles = nao // TILE
    slots_here = chol_tiles.shape[0]
    coef_tiles = orbitals.reshape(ntiles, TILE, norb)
    first = lax.axis_index("ao") * slots_here
    col_here = lax.dynamic_slice_in_dim(tile_col, first, slots_here)
    live_here = lax.dynamic_slice_in_dim(tile_live, first, slots_here)
    cols_coef = coef_tiles[col_here][:, :, :ACT]
    rows_coef = coef_tiles[tile_row]
    half = jnp.einsum("svmn,sna->vsam", chol_tiles, cols_coef, preferred_element_type=jnp.float32)
    half = (half * live_here.astype(jnp.float32)[None, :, None, None]).astype(jnp.bfloat16)
    received = lax.all_to_all(half, "ao", split_axis=0, concat_axis=1, tiled=True)
    b_vectors = jnp.einsum(
        "vsam,smp->vap", received, rows_coef, preferred_element_type=jnp.float32
    ).astype(jnp.bfloat16)
    vec_here = b_vectors.shape[0]
    flat = b_vectors[:, :, :ACT].reshape(vec_here, ACT * ACT)
    zeta = jnp.dot(flat, rdm_two, preferred_element_type=jnp.float32).reshape(vec_here, ACT, ACT)
    q_local = jnp.einsum(
        "vup,vtu->pt", b_vectors.astype(jnp.float32), zeta, precision=lax.Precision.HIGHEST
    )
    q_matrix = lax.psum(q_local, "ao")
    return (b_vectors, q_matrix)


def solution(mesh):
    return jax.shard_map(
        on_device,
        mesh=mesh,
        in_specs=(
            P(("grp", "ao"), None, None, None),
            P("grp", None),
            P("grp", None),
            P("grp"),
            P("grp"),
            P("grp"),
        ),
        out_specs=(P(("grp", "ao"), None, None), P("grp", None)),
        check_vma=False,
    )
```

```python
import functools

import jax
import jax.numpy as jnp
from jax import lax
from jax.experimental import pallas as pl
from jax.experimental.pallas import tpu as pltpu
from jax.sharding import PartitionSpec as P

TILE = 128
ACT = 40
MESH = pl.DeviceIdType.MESH
F32 = jnp.float32
BF16 = jnp.bfloat16
NT_DIMS = (((1,), (1,)), ((), ()))


def kernel(
    n, vec, norb, per, owners,
    row_ref, col_ref, live_ref, chol_hbm, orb_hbm, rdm_hbm,
    b_ref, q_ref,
    chol, orb_act, orb, rdm, sent, got, acc, zeta_t, q_parts, q_got, q_sum, q_full,
    load_sem, send_sem, recv_sem, rs_send, rs_recv, ag_send, ag_recv,
):
    me = lax.axis_index("ao")
    rows = vec * ACT
    flat_len = ACT * ACT
    lane_blocks = -(-norb // 128)
    owner_dev = [(o * n) // owners for o in range(owners)]

    loads = [
        pltpu.make_async_copy(orb_hbm.at[:, :, pl.ds(0, TILE)], orb_act, load_sem.at[0]),
        pltpu.make_async_copy(chol_hbm.at[0], chol, load_sem.at[1]),
        pltpu.make_async_copy(orb_hbm, orb, load_sem.at[2]),
        pltpu.make_async_copy(rdm_hbm, rdm, load_sem.at[3]),
    ]
    for load in loads:
        load.start()

    barrier = pltpu.get_barrier_semaphore()

    def greet(d, carry):
        pl.semaphore_signal(
            barrier, inc=1, device_id={"ao": lax.rem(me + d, n)}, device_id_type=MESH
        )
        return carry

    lax.fori_loop(1, n, greet, 0)

    q_parts[...] = jnp.zeros_like(q_parts)
    acc[...] = jnp.zeros_like(acc)
    live = live_ref[me].astype(F32)
    loads[0].wait()
    cols = orb_act[col_ref[me]]
    cols_t = jnp.transpose(cols.astype(F32))[:ACT].astype(BF16)
    loads[1].wait()

    def half(dest):
        tiles = chol[pl.ds(dest * vec, vec)].reshape(vec * TILE, TILE)
        out = lax.dot_general(cols_t, tiles, NT_DIMS, preferred_element_type=F32) * live
        parts = [out[:, v * TILE : (v + 1) * TILE] for v in range(vec)]
        return jnp.concatenate(parts, axis=0).astype(BF16)

    def distance(i):
        off = (i + 1) // 2
        return n // 2 + off * (2 * ((i + 1) % 2) - 1)

    def slot_copy(there, mine):
        return pltpu.make_async_remote_copy(
            src_ref=sent.at[there],
            dst_ref=got.at[mine],
            send_sem=send_sem.at[there],
            recv_sem=recv_sem.at[mine],
            device_id={"ao": there},
            device_id_type=MESH,
        )

    far = lax.rem(me + n // 2, n)
    sent[far] = half(far)
    pl.semaphore_wait(barrier, n - 1)
    slot_copy(far, me).start()

    def send_step(i, carry):
        dest = lax.rem(me + distance(i), n)
        sent[dest] = half(dest)
        slot_copy(dest, me).start()
        return carry

    lax.fori_loop(1, n - 1, send_step, 0, unroll=n <= 16)

    own = half(me)
    column = lax.broadcasted_iota(jnp.int32, (1, flat_len), 1)
    lane_of = column - (column // ACT) * ACT
    pick = (lax.broadcasted_iota(jnp.int32, (TILE, flat_len), 0) == lane_of).astype(F32).astype(BF16)
    mask = lax.broadcasted_iota(jnp.int32, (ACT, flat_len), 0) == column // ACT
    loads[2].wait()

    def coef(slot):
        return orb[row_ref[slot]]

    acc[...] += jnp.dot(own, coef(me), preferred_element_type=F32)

    def take_step(j, carry):
        src = lax.rem(me + n - distance(n - 2 - j), n)
        pltpu.make_async_remote_copy(
            src_ref=sent.at[src],
            dst_ref=got.at[src],
            send_sem=send_sem.at[src],
            recv_sem=recv_sem.at[src],
            device_id={"ao": src},
            device_id_type=MESH,
        ).wait_recv()
        acc[...] += jnp.dot(got[src], coef(src), preferred_element_type=F32)
        return carry

    lax.fori_loop(0, n - 1, take_step, 0, unroll=n <= 16)

    b16 = acc[...].astype(BF16)
    b_ref[...] = b16
    spread = jnp.dot(b16[:, :TILE], pick, preferred_element_type=F32)
    flat = jnp.concatenate(
        [
            jnp.sum(jnp.where(mask, spread[v * ACT : (v + 1) * ACT], 0.0), axis=0, keepdims=True)
            for v in range(vec)
        ],
        axis=0,
    ).astype(BF16)
    loads[3].wait()
    zeta = jnp.dot(flat, rdm[...], preferred_element_type=F32)
    for t in range(ACT):
        zeta_t[t] = zeta[:, t * ACT : (t + 1) * ACT]
    b32 = b16.astype(F32)
    q_t = jnp.zeros((ACT, norb), F32)
    for v in range(vec):
        z = zeta_t[:, v, :]
        high = z.astype(BF16)
        low = (z - high.astype(F32)).astype(BF16)
        b_v = b32[v * ACT : (v + 1) * ACT].astype(BF16)
        q_t += jnp.dot(high, b_v, preferred_element_type=F32)
        q_t += jnp.dot(low, b_v, preferred_element_type=F32)

    def block_of(k):
        r, c = k // lane_blocks, k % lane_blocks
        return r * 8, c * 128, min(128, norb - c * 128)

    blocks = (ACT // 8) * lane_blocks
    for k in range(blocks):
        r, c, wide = block_of(k)
        q_parts[k // per, k % per, :, pl.ds(0, wide)] = q_t[r : r + 8, c : c + wide]

    def rs_copy(o):
        return pltpu.make_async_remote_copy(
            src_ref=q_parts.at[o],
            dst_ref=q_got.at[me],
            send_sem=rs_send.at[o],
            recv_sem=rs_recv.at[me],
            device_id={"ao": owner_dev[o]},
            device_id_type=MESH,
        )

    def ag_copy(o, dest):
        return pltpu.make_async_remote_copy(
            src_ref=q_sum,
            dst_ref=q_full.at[o],
            send_sem=ag_send.at[dest],
            recv_sem=ag_recv.at[o],
            device_id={"ao": dest},
            device_id_type=MESH,
        )

    for o in range(owners):
        @pl.when(me != owner_dev[o])
        def _():
            rs_copy(o).start()

    for o in range(owners):
        @pl.when(me == owner_dev[o])
        def _():
            q_sum[...] = q_parts[o]

            def add_step(d, carry):
                src = lax.rem(me + d, n)
                pltpu.make_async_remote_copy(
                    src_ref=q_parts.at[o],
                    dst_ref=q_got.at[src],
                    send_sem=rs_send.at[o],
                    recv_sem=rs_recv.at[src],
                    device_id={"ao": src},
                    device_id_type=MESH,
                ).wait_recv()
                q_sum[...] += q_got[src]
                return carry

            lax.fori_loop(1, n, add_step, 0)

            def spread_step(d, carry):
                ag_copy(o, lax.rem(me + d, n)).start()
                return carry

            lax.fori_loop(1, n, spread_step, 0)
            q_full[o] = q_sum[...]

    for o in range(owners):
        @pl.when(me != owner_dev[o])
        def _():
            ag_copy(o, owner_dev[o]).wait_recv()

    for k in range(blocks):
        r, c, wide = block_of(k)
        q_ref[pl.ds(r, 8), pl.ds(c, wide)] = q_full[k // per, k % per, :, pl.ds(0, wide)]

    def drain(d, carry):
        dest = lax.rem(me + d, n)
        slot_copy(dest, me).wait_send()
        return carry

    lax.fori_loop(1, n, drain, 0)
    for o in range(owners):
        @pl.when(me != owner_dev[o])
        def _():
            rs_copy(o).wait_send()

        @pl.when(me == owner_dev[o])
        def _():
            def done(d, carry):
                ag_copy(o, lax.rem(me + d, n)).wait_send()
                return carry

            lax.fori_loop(1, n, done, 0)


def solution(mesh):
    n = mesh.shape["ao"]

    def on_device(chol_tiles, orbitals, rdm_two, tile_row, tile_col, tile_live):
        nao, norb = orbitals.shape
        vec_all = chol_tiles.shape[1]
        vec = vec_all // n
        rows = vec * ACT
        blocks = (ACT // 8) * (-(-norb // 128))
        per = -(-blocks // n)
        owners = -(-blocks // per)
        b, q_t = pl.pallas_call(
            functools.partial(kernel, n, vec, norb, per, owners),
            out_shape=(
                jax.ShapeDtypeStruct((rows, norb), BF16),
                jax.ShapeDtypeStruct((ACT, norb), F32),
            ),
            in_specs=[pl.BlockSpec(memory_space=pltpu.SMEM)] * 3
            + [pl.BlockSpec(memory_space=pl.ANY)] * 3,
            out_specs=(
                pl.BlockSpec(memory_space=pltpu.VMEM),
                pl.BlockSpec(memory_space=pltpu.VMEM),
            ),
            scratch_shapes=[
                pltpu.VMEM((vec_all, TILE, TILE), BF16),
                pltpu.VMEM((nao // TILE, TILE, TILE), BF16),
                pltpu.VMEM((nao // TILE, TILE, norb), BF16),
                pltpu.VMEM(rdm_two.shape, BF16),
                pltpu.VMEM((n, rows, TILE), BF16),
                pltpu.VMEM((n, rows, TILE), BF16),
                pltpu.VMEM((rows, norb), F32),
                pltpu.VMEM((ACT, vec, ACT), F32),
                pltpu.VMEM((owners, per, 8, 128), F32),
                pltpu.VMEM((n, per, 8, 128), F32),
                pltpu.VMEM((per, 8, 128), F32),
                pltpu.VMEM((owners, per, 8, 128), F32),
                pltpu.SemaphoreType.DMA((4,)),
                pltpu.SemaphoreType.DMA((n,)),
                pltpu.SemaphoreType.DMA((n,)),
                pltpu.SemaphoreType.DMA((owners,)),
                pltpu.SemaphoreType.DMA((n,)),
                pltpu.SemaphoreType.DMA((n,)),
                pltpu.SemaphoreType.DMA((owners,)),
            ],
            compiler_params=pltpu.CompilerParams(
                collective_id=0, has_side_effects=True, vmem_limit_bytes=56 * 1024 * 1024
            ),
        )(
            tile_row, tile_col, tile_live, chol_tiles,
            orbitals.reshape(nao // TILE, TILE, norb), rdm_two,
        )
        return b.reshape(vec, ACT, norb), q_t.T

    return jax.shard_map(
        on_device,
        mesh=mesh,
        in_specs=(
            P(("grp", "ao"), None, None, None),
            P("grp", None),
            P("grp", None),
            P("grp"),
            P("grp"),
            P("grp"),
        ),
        out_specs=(P(("grp", "ao"), None, None), P("grp", None)),
        check_vma=False,
    )
```

```python
import functools

import jax
import jax.numpy as jnp
from jax import lax
from jax.experimental import pallas as pl
from jax.experimental.pallas import tpu as pltpu
from jax.sharding import PartitionSpec as P

TILE = 128
ACT = 40
ACT_ROWS = 48
MESH = pl.DeviceIdType.MESH
F32 = jnp.float32
BF16 = jnp.bfloat16
NT_DIMS = (((1,), (1,)), ((), ()))


def kernel(
    n, vec, norb, per, owners,
    row_ref, col_ref, live_ref, chol_hbm, orb_hbm, rdm_hbm,
    b_ref, q_ref,
    chol, act_wide, act, orb, rdm, sent, got, acc, zeta_t, q_parts, q_got, q_sum, q_full,
    load_sem, send_sem, recv_sem, rs_send, rs_recv, ag_send, ag_recv,
):
    me = lax.axis_index("ao")
    rows = vec * ACT
    flat_len = ACT * ACT
    lane_blocks = -(-norb // 128)
    owner_dev = [(o * n) // owners for o in range(owners)]

    loads = [
        pltpu.make_async_copy(orb_hbm.at[pl.ds(0, ACT_ROWS)], act_wide, load_sem.at[0]),
        pltpu.make_async_copy(chol_hbm.at[0], chol, load_sem.at[1]),
        pltpu.make_async_copy(rdm_hbm, rdm, load_sem.at[2]),
    ]
    loads[0].start()
    loads[1].start()
    ntiles = orb.shape[0]

    barrier = pltpu.get_barrier_semaphore()

    def greet(d, carry):
        pl.semaphore_signal(
            barrier, inc=1, device_id={"ao": lax.rem(me + d, n)}, device_id_type=MESH
        )
        return carry

    lax.fori_loop(1, n, greet, 0)

    q_parts[...] = jnp.zeros_like(q_parts)
    live = live_ref[me].astype(F32)
    loads[0].wait()
    for k in range(ntiles):
        act[k] = act_wide[:, k * TILE : (k + 1) * TILE]
    cols_t = act[col_ref[me]]
    loads[1].wait()

    def half(dest):
        tiles = chol[pl.ds(dest * vec, vec)].reshape(vec * TILE, TILE)
        out = lax.dot_general(cols_t, tiles, NT_DIMS, preferred_element_type=F32)
        out = out[:ACT] * live
        parts = [out[:, v * TILE : (v + 1) * TILE] for v in range(vec)]
        return jnp.concatenate(parts, axis=0).astype(BF16)

    def distance(i):
        off = (i + 1) // 2
        return n // 2 + off * (2 * ((i + 1) % 2) - 1)

    def slot_copy(there, mine):
        return pltpu.make_async_remote_copy(
            src_ref=sent.at[there],
            dst_ref=got.at[mine],
            send_sem=send_sem.at[there],
            recv_sem=recv_sem.at[mine],
            device_id={"ao": there},
            device_id_type=MESH,
        )

    far = lax.rem(me + n // 2, n)
    sent[far] = half(far)
    pl.semaphore_wait(barrier, n - 1)
    slot_copy(far, me).start()
    for k in range(ntiles):
        pltpu.make_async_copy(
            orb_hbm.at[:, pl.ds(k * TILE, TILE)], orb.at[k], load_sem.at[3]
        ).start()
    loads[2].start()

    def send_step(i, carry):
        dest = lax.rem(me + distance(i), n)
        sent[dest] = half(dest)
        slot_copy(dest, me).start()
        return carry

    lax.fori_loop(1, n - 1, send_step, 0, unroll=n <= 16)

    own = half(me)
    column = lax.broadcasted_iota(jnp.int32, (1, flat_len), 1)
    lane_of = column - (column // ACT) * ACT
    pick = (lax.broadcasted_iota(jnp.int32, (TILE, flat_len), 0) == lane_of).astype(F32).astype(BF16)
    mask = lax.broadcasted_iota(jnp.int32, (ACT, flat_len), 0) == column // ACT
    pltpu.make_async_copy(orb, orb, load_sem.at[3]).wait()

    def second(block, slot):
        return lax.dot_general(block, orb[row_ref[slot]], NT_DIMS, preferred_element_type=F32)

    acc[...] = second(own, me)

    def take_step(j, carry):
        src = lax.rem(me + n - distance(n - 2 - j), n)
        pltpu.make_async_remote_copy(
            src_ref=sent.at[src],
            dst_ref=got.at[src],
            send_sem=send_sem.at[src],
            recv_sem=recv_sem.at[src],
            device_id={"ao": src},
            device_id_type=MESH,
        ).wait_recv()
        acc[...] += second(got[src], src)
        return carry

    lax.fori_loop(0, n - 1, take_step, 0, unroll=n <= 16)

    b16 = acc[...].astype(BF16)
    b_ref[...] = b16
    spread = jnp.dot(b16[:, :TILE], pick, preferred_element_type=F32)
    flat = jnp.concatenate(
        [
            jnp.sum(jnp.where(mask, spread[v * ACT : (v + 1) * ACT], 0.0), axis=0, keepdims=True)
            for v in range(vec)
        ],
        axis=0,
    ).astype(BF16)
    loads[2].wait()
    zeta = jnp.dot(flat, rdm[...], preferred_element_type=F32)
    for t in range(ACT):
        zeta_t[t] = zeta[:, t * ACT : (t + 1) * ACT]
    b32 = b16.astype(F32)
    q_t = jnp.zeros((ACT, norb), F32)
    for v in range(vec):
        z = zeta_t[:, v, :]
        high = z.astype(BF16)
        low = (z - high.astype(F32)).astype(BF16)
        b_v = b32[v * ACT : (v + 1) * ACT].astype(BF16)
        q_t += jnp.dot(high, b_v, preferred_element_type=F32)
        q_t += jnp.dot(low, b_v, preferred_element_type=F32)

    def block_of(k):
        r, c = k // lane_blocks, k % lane_blocks
        return r * 8, c * 128, min(128, norb - c * 128)

    blocks = (ACT // 8) * lane_blocks
    for k in range(blocks):
        r, c, wide = block_of(k)
        q_parts[k // per, k % per, :, pl.ds(0, wide)] = q_t[r : r + 8, c : c + wide]

    def rs_copy(o):
        return pltpu.make_async_remote_copy(
            src_ref=q_parts.at[o],
            dst_ref=q_got.at[me],
            send_sem=rs_send.at[o],
            recv_sem=rs_recv.at[me],
            device_id={"ao": owner_dev[o]},
            device_id_type=MESH,
        )

    def ag_copy(o, dest):
        return pltpu.make_async_remote_copy(
            src_ref=q_sum,
            dst_ref=q_full.at[o],
            send_sem=ag_send.at[dest],
            recv_sem=ag_recv.at[o],
            device_id={"ao": dest},
            device_id_type=MESH,
        )

    for o in range(owners):
        @pl.when(me != owner_dev[o])
        def _():
            rs_copy(o).start()

    for o in range(owners):
        @pl.when(me == owner_dev[o])
        def _():
            q_sum[...] = q_parts[o]

            def add_step(d, carry):
                src = lax.rem(me + d, n)
                pltpu.make_async_remote_copy(
                    src_ref=q_parts.at[o],
                    dst_ref=q_got.at[src],
                    send_sem=rs_send.at[o],
                    recv_sem=rs_recv.at[src],
                    device_id={"ao": src},
                    device_id_type=MESH,
                ).wait_recv()
                q_sum[...] += q_got[src]
                return carry

            lax.fori_loop(1, n, add_step, 0)

            def spread_step(d, carry):
                ag_copy(o, lax.rem(me + d, n)).start()
                return carry

            lax.fori_loop(1, n, spread_step, 0)
            q_full[o] = q_sum[...]

    for o in range(owners):
        @pl.when(me != owner_dev[o])
        def _():
            ag_copy(o, owner_dev[o]).wait_recv()

    for k in range(blocks):
        r, c, wide = block_of(k)
        q_ref[pl.ds(r, 8), pl.ds(c, wide)] = q_full[k // per, k % per, :, pl.ds(0, wide)]

    def drain(d, carry):
        dest = lax.rem(me + d, n)
        slot_copy(dest, me).wait_send()
        return carry

    lax.fori_loop(1, n, drain, 0)
    for o in range(owners):
        @pl.when(me != owner_dev[o])
        def _():
            rs_copy(o).wait_send()

        @pl.when(me == owner_dev[o])
        def _():
            def done(d, carry):
                ag_copy(o, lax.rem(me + d, n)).wait_send()
                return carry

            lax.fori_loop(1, n, done, 0)


def solution(mesh):
    n = mesh.shape["ao"]

    def on_device(chol_tiles, orbitals, rdm_two, tile_row, tile_col, tile_live):
        nao, norb = orbitals.shape
        vec_all = chol_tiles.shape[1]
        vec = vec_all // n
        rows = vec * ACT
        blocks = (ACT // 8) * (-(-norb // 128))
        per = -(-blocks // n)
        owners = -(-blocks // per)
        b, q_t = pl.pallas_call(
            functools.partial(kernel, n, vec, norb, per, owners),
            out_shape=(
                jax.ShapeDtypeStruct((rows, norb), BF16),
                jax.ShapeDtypeStruct((ACT, norb), F32),
            ),
            in_specs=[pl.BlockSpec(memory_space=pltpu.SMEM)] * 3
            + [pl.BlockSpec(memory_space=pl.ANY)] * 3,
            out_specs=(
                pl.BlockSpec(memory_space=pltpu.VMEM),
                pl.BlockSpec(memory_space=pltpu.VMEM),
            ),
            scratch_shapes=[
                pltpu.VMEM((vec_all, TILE, TILE), BF16),
                pltpu.VMEM((ACT_ROWS, nao), BF16),
                pltpu.VMEM((nao // TILE, ACT_ROWS, TILE), BF16),
                pltpu.VMEM((nao // TILE, norb, TILE), BF16),
                pltpu.VMEM(rdm_two.shape, BF16),
                pltpu.VMEM((n, rows, TILE), BF16),
                pltpu.VMEM((n, rows, TILE), BF16),
                pltpu.VMEM((rows, norb), F32),
                pltpu.VMEM((ACT, vec, ACT), F32),
                pltpu.VMEM((owners, per, 8, 128), F32),
                pltpu.VMEM((n, per, 8, 128), F32),
                pltpu.VMEM((per, 8, 128), F32),
                pltpu.VMEM((owners, per, 8, 128), F32),
                pltpu.SemaphoreType.DMA((4,)),
                pltpu.SemaphoreType.DMA((n,)),
                pltpu.SemaphoreType.DMA((n,)),
                pltpu.SemaphoreType.DMA((owners,)),
                pltpu.SemaphoreType.DMA((n,)),
                pltpu.SemaphoreType.DMA((n,)),
                pltpu.SemaphoreType.DMA((owners,)),
            ],
            compiler_params=pltpu.CompilerParams(
                collective_id=0, has_side_effects=True, vmem_limit_bytes=56 * 1024 * 1024
            ),
        )(
            tile_row, tile_col, tile_live, chol_tiles,
            orbitals.T, rdm_two,
        )
        return b.reshape(vec, ACT, norb), q_t.T

    return jax.shard_map(
        on_device,
        mesh=mesh,
        in_specs=(
            P(("grp", "ao"), None, None, None),
            P("grp", None),
            P("grp", None),
            P("grp"),
            P("grp"),
            P("grp"),
        ),
        out_specs=(P(("grp", "ao"), None, None), P("grp", None)),
        check_vma=False,
    )
```

```python
import functools

import jax
import jax.numpy as jnp
from jax import lax
from jax.experimental import pallas as pl
from jax.experimental.pallas import tpu as pltpu
from jax.sharding import PartitionSpec as P

TILE = 128
ACT = 40
ACT_ROWS = 48
MESH = pl.DeviceIdType.MESH
F32 = jnp.float32
BF16 = jnp.bfloat16
NT_DIMS = (((1,), (1,)), ((), ()))


def kernel(
    n, inner, vec, norb, per,
    row_ref, col_ref, live_ref, chol_hbm, orb_hbm, rdm_hbm,
    b_ref, q_ref,
    chol, act_wide, act, orb, rdm, sent, got, acc, zeta_t,
    q_parts, q_got, q_line, q_full, b_vmem, q_vmem,
    load_sem, send_sem, recv_sem, s1_send, s1_recv, s2_send, s2_recv, s3_send, s3_recv,
):
    me = lax.axis_index("ao")
    rows = vec * ACT
    flat_len = ACT * ACT

    loads = [
        pltpu.make_async_copy(orb_hbm.at[pl.ds(0, ACT_ROWS)], act_wide, load_sem.at[0]),
        pltpu.make_async_copy(chol_hbm.at[0], chol, load_sem.at[1]),
        pltpu.make_async_copy(rdm_hbm, rdm, load_sem.at[2]),
    ]
    loads[0].start()
    loads[1].start()
    ntiles = orb.shape[0]

    barrier = pltpu.get_barrier_semaphore()

    def greet(d, carry):
        pl.semaphore_signal(
            barrier, inc=1, device_id={"ao": lax.rem(me + d, n)}, device_id_type=MESH
        )
        return carry

    lax.fori_loop(1, n, greet, 0, unroll=n <= 16)

    q_parts[...] = jnp.zeros_like(q_parts)
    live = live_ref[me].astype(F32)
    loads[0].wait()
    for k in range(ntiles):
        act[k] = act_wide[:, k * TILE : (k + 1) * TILE]
    cols_t = act[col_ref[me]]
    loads[1].wait()

    def half(dest):
        tiles = chol[pl.ds(dest * vec, vec)].reshape(vec * TILE, TILE)
        out = lax.dot_general(cols_t, tiles, NT_DIMS, preferred_element_type=F32)
        out = out[:ACT] * live
        parts = [out[:, v * TILE : (v + 1) * TILE] for v in range(vec)]
        return jnp.concatenate(parts, axis=0).astype(BF16)

    def distance(i):
        off = (i + 1) // 2
        return n // 2 + off * (2 * ((i + 1) % 2) - 1)

    def slot_copy(there, mine):
        return pltpu.make_async_remote_copy(
            src_ref=sent.at[there],
            dst_ref=got.at[mine],
            send_sem=send_sem.at[there],
            recv_sem=recv_sem.at[mine],
            device_id={"ao": there},
            device_id_type=MESH,
        )

    far = lax.rem(me + n // 2, n)
    sent[far] = half(far)
    pl.semaphore_wait(barrier, n - 1)
    slot_copy(far, me).start()
    for k in range(ntiles):
        pltpu.make_async_copy(
            orb_hbm.at[:, pl.ds(k * TILE, TILE)], orb.at[k], load_sem.at[3]
        ).start()
    loads[2].start()

    def send_step(i, carry):
        dest = lax.rem(me + distance(i), n)
        sent[dest] = half(dest)
        slot_copy(dest, me).start()
        return carry

    lax.fori_loop(1, n - 1, send_step, 0, unroll=n <= 16)

    own = half(me)
    column = lax.broadcasted_iota(jnp.int32, (1, flat_len), 1)
    lane_of = column - (column // ACT) * ACT
    pick = (lax.broadcasted_iota(jnp.int32, (TILE, flat_len), 0) == lane_of).astype(F32).astype(BF16)
    mask = lax.broadcasted_iota(jnp.int32, (ACT, flat_len), 0) == column // ACT
    pltpu.make_async_copy(orb, orb, load_sem.at[3]).wait()

    def second(block, slot):
        return lax.dot_general(block, orb[row_ref[slot]], NT_DIMS, preferred_element_type=F32)

    acc[...] = second(own, me)

    def take_step(j, carry):
        src = lax.rem(me + n - distance(n - 2 - j), n)
        pltpu.make_async_remote_copy(
            src_ref=sent.at[src],
            dst_ref=got.at[src],
            send_sem=send_sem.at[src],
            recv_sem=recv_sem.at[src],
            device_id={"ao": src},
            device_id_type=MESH,
        ).wait_recv()
        acc[...] += second(got[src], src)
        return carry

    lax.fori_loop(0, n - 1, take_step, 0, unroll=n <= 16)

    b16 = acc[...].astype(BF16)
    b_vmem[...] = b16
    b_out = pltpu.make_async_copy(b_vmem, b_ref, load_sem.at[0])
    b_out.start()
    spread = jnp.dot(b16[:, :TILE], pick, preferred_element_type=F32)
    flat = jnp.concatenate(
        [
            jnp.sum(jnp.where(mask, spread[v * ACT : (v + 1) * ACT], 0.0), axis=0, keepdims=True)
            for v in range(vec)
        ],
        axis=0,
    ).astype(BF16)
    loads[2].wait()
    zeta = jnp.dot(flat, rdm[...], preferred_element_type=F32)
    for t in range(ACT):
        zeta_t[t] = zeta[:, t * ACT : (t + 1) * ACT]
    b32 = b16.astype(F32)
    q_t = jnp.zeros((ACT, norb), F32)
    for v in range(vec):
        z = zeta_t[:, v, :]
        high = z.astype(BF16)
        low = (z - high.astype(F32)).astype(BF16)
        b_v = b32[v * ACT : (v + 1) * ACT].astype(BF16)
        q_t += jnp.dot(high, b_v, preferred_element_type=F32)
        q_t += jnp.dot(low, b_v, preferred_element_type=F32)

    tiles_of = [
        (r, c, min(128, norb - c)) for r in range(0, ACT, 8) for c in range(0, norb, 128)
    ]
    for k, (r, c, wide) in enumerate(tiles_of):
        q_parts[k // per, k % per, :, pl.ds(0, wide)] = q_t[r : r + 8, c : c + wide]

    plane, spot = me // inner, lax.rem(me, inner)
    outer = n // inner

    def scatter(e):
        there = lax.rem(spot + e, inner)
        return pltpu.make_async_remote_copy(
            src_ref=q_parts.at[there],
            dst_ref=q_got.at[e - 1],
            send_sem=s1_send.at[e - 1],
            recv_sem=s1_recv.at[e - 1],
            device_id={"ao": plane * inner + there},
            device_id_type=MESH,
        )

    def exchange(e, slot):
        return pltpu.make_async_remote_copy(
            src_ref=q_line.at[slot],
            dst_ref=q_line.at[slot],
            send_sem=s2_send.at[e - 1],
            recv_sem=s2_recv.at[slot],
            device_id={"ao": lax.rem(plane + e, outer) * inner + spot},
            device_id_type=MESH,
        )

    def gather(e, slot):
        return pltpu.make_async_remote_copy(
            src_ref=q_full.at[slot],
            dst_ref=q_full.at[slot],
            send_sem=s3_send.at[e - 1],
            recv_sem=s3_recv.at[slot],
            device_id={"ao": plane * inner + lax.rem(spot + e, inner)},
            device_id_type=MESH,
        )

    for e in range(1, inner):
        scatter(e).start()
    part = q_parts[spot]
    for e in range(1, inner):
        scatter(e).wait_recv()
        part += q_got[e - 1]
    q_line[plane] = part
    for e in range(1, outer):
        exchange(e, plane).start()
    for e in range(1, outer):
        exchange(e, lax.rem(plane + outer - e, outer)).wait_recv()
    total = q_line[0]
    for z in range(1, outer):
        total += q_line[z]
    q_full[spot] = total
    for e in range(1, inner):
        gather(e, spot).start()
    for e in range(1, inner):
        gather(e, lax.rem(spot + inner - e, inner)).wait_recv()

    for k, (r, c, wide) in enumerate(tiles_of):
        q_vmem[pl.ds(r, 8), pl.ds(c, wide)] = q_full[k // per, k % per, :, pl.ds(0, wide)]
    q_out = pltpu.make_async_copy(q_vmem, q_ref, load_sem.at[1])
    q_out.start()

    def drain(d, carry):
        slot_copy(lax.rem(me + d, n), me).wait_send()
        return carry

    lax.fori_loop(1, n, drain, 0)
    for e in range(1, inner):
        scatter(e).wait_send()
        gather(e, spot).wait_send()
    for e in range(1, outer):
        exchange(e, plane).wait_send()
    b_out.wait()
    q_out.wait()


def hand_over(b_in, q_in, b_ref, q_ref, sems):
    copies = [
        pltpu.make_async_copy(b_in, b_ref, sems.at[0]),
        pltpu.make_async_copy(q_in, q_ref, sems.at[1]),
    ]
    for copy in copies:
        copy.start()
    for copy in copies:
        copy.wait()


def solution(mesh):
    n = mesh.shape["ao"]

    def on_device(chol_tiles, orbitals, rdm_two, tile_row, tile_col, tile_live):
        nao, norb = orbitals.shape
        vec_all = chol_tiles.shape[1]
        vec = vec_all // n
        rows = vec * ACT
        blocks = (ACT // 8) * (-(-norb // 128))
        inner = 4 if n % 4 == 0 else 1
        outer = n // inner
        per = -(-blocks // inner)
        b, q_t = pl.pallas_call(
            functools.partial(kernel, n, inner, vec, norb, per),
            out_shape=(
                jax.ShapeDtypeStruct((rows, norb), BF16),
                jax.ShapeDtypeStruct((ACT, norb), F32),
            ),
            in_specs=[pl.BlockSpec(memory_space=pltpu.SMEM)] * 3
            + [pl.BlockSpec(memory_space=pl.ANY)] * 3,
            out_specs=(pl.BlockSpec(memory_space=pl.ANY),) * 2,
            scratch_shapes=[
                pltpu.VMEM((vec_all, TILE, TILE), BF16),
                pltpu.VMEM((ACT_ROWS, nao), BF16),
                pltpu.VMEM((nao // TILE, ACT_ROWS, TILE), BF16),
                pltpu.VMEM((nao // TILE, norb, TILE), BF16),
                pltpu.VMEM(rdm_two.shape, BF16),
                pltpu.VMEM((n, rows, TILE), BF16),
                pltpu.VMEM((n, rows, TILE), BF16),
                pltpu.VMEM((rows, norb), F32),
                pltpu.VMEM((ACT, vec, ACT), F32),
                pltpu.VMEM((inner, per, 8, 128), F32),
                pltpu.VMEM((inner, per, 8, 128), F32),
                pltpu.VMEM((outer, per, 8, 128), F32),
                pltpu.VMEM((inner, per, 8, 128), F32),
                pltpu.VMEM((rows, norb), BF16),
                pltpu.VMEM((ACT, norb), F32),
                pltpu.SemaphoreType.DMA((4,)),
                pltpu.SemaphoreType.DMA((n,)),
                pltpu.SemaphoreType.DMA((n,)),
                pltpu.SemaphoreType.DMA((inner,)),
                pltpu.SemaphoreType.DMA((inner,)),
                pltpu.SemaphoreType.DMA((outer,)),
                pltpu.SemaphoreType.DMA((outer,)),
                pltpu.SemaphoreType.DMA((inner,)),
                pltpu.SemaphoreType.DMA((inner,)),
            ],
            compiler_params=pltpu.CompilerParams(
                collective_id=0, has_side_effects=True, vmem_limit_bytes=56 * 1024 * 1024
            ),
        )(
            tile_row, tile_col, tile_live, chol_tiles,
            orbitals.T, rdm_two,
        )
        b, q_t = pl.pallas_call(
            hand_over,
            out_shape=(
                jax.ShapeDtypeStruct((rows, norb), BF16),
                jax.ShapeDtypeStruct((ACT, norb), F32),
            ),
            in_specs=[pl.BlockSpec(memory_space=pl.ANY)] * 2,
            out_specs=(pl.BlockSpec(memory_space=pl.ANY),) * 2,
            scratch_shapes=[pltpu.SemaphoreType.DMA((2,))],
            compiler_params=pltpu.CompilerParams(vmem_limit_bytes=56 * 1024 * 1024),
        )(b, q_t)
        return b.reshape(vec, ACT, norb), q_t.T

    return jax.shard_map(
        on_device,
        mesh=mesh,
        in_specs=(
            P(("grp", "ao"), None, None, None),
            P("grp", None),
            P("grp", None),
            P("grp"),
            P("grp"),
            P("grp"),
        ),
        out_specs=(P(("grp", "ao"), None, None), P("grp", None)),
        check_vma=False,
    )
```

```python
import functools

import jax
import jax.numpy as jnp
from jax import lax
from jax.experimental import pallas as pl
from jax.experimental.pallas import tpu as pltpu
from jax.sharding import PartitionSpec as P

TILE = 128
ACT = 40
ACT_ROWS = 48
MESH = pl.DeviceIdType.MESH
F32 = jnp.float32
BF16 = jnp.bfloat16
NT_DIMS = (((1,), (1,)), ((), ()))


def kernel(
    n, vec, norb, per, owners,
    row_ref, col_ref, live_ref, chol_hbm, orb_hbm, rdm_hbm,
    b_ref, q_ref,
    chol, act_wide, act, orb, rdm, sent, got, acc, zeta_t, q_parts, q_got, q_sum, q_full,
    load_sem, send_sem, recv_sem, rs_send, rs_recv, ag_send, ag_recv,
):
    me = lax.axis_index("ao")
    rows = vec * ACT
    flat_len = ACT * ACT
    lane_blocks = -(-norb // 128)
    owner_dev = [(o * n) // owners for o in range(owners)]

    loads = [
        pltpu.make_async_copy(orb_hbm.at[pl.ds(0, ACT_ROWS)], act_wide, load_sem.at[0]),
        pltpu.make_async_copy(chol_hbm.at[0], chol, load_sem.at[1]),
        pltpu.make_async_copy(rdm_hbm, rdm, load_sem.at[2]),
    ]
    loads[0].start()
    loads[1].start()
    ntiles = orb.shape[0]

    barrier = pltpu.get_barrier_semaphore()

    def greet(d, carry):
        pl.semaphore_signal(
            barrier, inc=1, device_id={"ao": lax.rem(me + d, n)}, device_id_type=MESH
        )
        return carry

    lax.fori_loop(1, n, greet, 0)

    q_parts[...] = jnp.zeros_like(q_parts)
    live = live_ref[me].astype(F32)
    loads[0].wait()
    for k in range(ntiles):
        act[k] = act_wide[:, k * TILE : (k + 1) * TILE]
    cols_t = act[col_ref[me]]
    loads[1].wait()

    def half(dest):
        tiles = chol[pl.ds(dest * vec, vec)].reshape(vec * TILE, TILE)
        out = lax.dot_general(cols_t, tiles, NT_DIMS, preferred_element_type=F32)
        out = out[:ACT] * live
        parts = [out[:, v * TILE : (v + 1) * TILE] for v in range(vec)]
        return jnp.concatenate(parts, axis=0).astype(BF16)

    def distance(i):
        off = (i + 1) // 2
        return n // 2 + off * (2 * ((i + 1) % 2) - 1)

    def slot_copy(there, mine):
        return pltpu.make_async_remote_copy(
            src_ref=sent.at[there],
            dst_ref=got.at[mine],
            send_sem=send_sem.at[there],
            recv_sem=recv_sem.at[mine],
            device_id={"ao": there},
            device_id_type=MESH,
        )

    far = lax.rem(me + n // 2, n)
    sent[far] = half(far)
    pl.semaphore_wait(barrier, n - 1)
    slot_copy(far, me).start()
    for k in range(ntiles):
        pltpu.make_async_copy(
            orb_hbm.at[:, pl.ds(k * TILE, TILE)], orb.at[k], load_sem.at[3]
        ).start()
    loads[2].start()

    def send_step(i, carry):
        dest = lax.rem(me + distance(i), n)
        sent[dest] = half(dest)
        slot_copy(dest, me).start()
        return carry

    lax.fori_loop(1, n - 1, send_step, 0, unroll=n <= 16)

    own = half(me)
    column = lax.broadcasted_iota(jnp.int32, (1, flat_len), 1)
    lane_of = column - (column // ACT) * ACT
    pick = (lax.broadcasted_iota(jnp.int32, (TILE, flat_len), 0) == lane_of).astype(F32).astype(BF16)
    mask = lax.broadcasted_iota(jnp.int32, (ACT, flat_len), 0) == column // ACT
    pltpu.make_async_copy(orb, orb, load_sem.at[3]).wait()

    def second(block, slot):
        return lax.dot_general(block, orb[row_ref[slot]], NT_DIMS, preferred_element_type=F32)

    acc[...] = second(own, me)

    def take_step(j, carry):
        src = lax.rem(me + n - distance(n - 2 - j), n)
        pltpu.make_async_remote_copy(
            src_ref=sent.at[src],
            dst_ref=got.at[src],
            send_sem=send_sem.at[src],
            recv_sem=recv_sem.at[src],
            device_id={"ao": src},
            device_id_type=MESH,
        ).wait_recv()
        acc[...] += second(got[src], src)
        return carry

    lax.fori_loop(0, n - 1, take_step, 0, unroll=n <= 16)

    b16 = acc[...].astype(BF16)
    b_ref[...] = b16
    spread = jnp.dot(b16[:, :TILE], pick, preferred_element_type=F32)
    flat = jnp.concatenate(
        [
            jnp.sum(jnp.where(mask, spread[v * ACT : (v + 1) * ACT], 0.0), axis=0, keepdims=True)
            for v in range(vec)
        ],
        axis=0,
    ).astype(BF16)
    loads[2].wait()
    zeta = jnp.dot(flat, rdm[...], preferred_element_type=F32)
    for t in range(ACT):
        zeta_t[t] = zeta[:, t * ACT : (t + 1) * ACT]
    b32 = b16.astype(F32)
    q_t = jnp.zeros((ACT, norb), F32)
    for v in range(vec):
        z = zeta_t[:, v, :]
        high = z.astype(BF16)
        low = (z - high.astype(F32)).astype(BF16)
        b_v = b32[v * ACT : (v + 1) * ACT].astype(BF16)
        q_t += jnp.dot(high, b_v, preferred_element_type=F32)
        q_t += jnp.dot(low, b_v, preferred_element_type=F32)

    def block_of(k):
        r, c = k // lane_blocks, k % lane_blocks
        return r * 8, c * 128, min(128, norb - c * 128)

    blocks = (ACT // 8) * lane_blocks
    for k in range(blocks):
        r, c, wide = block_of(k)
        q_parts[k // per, k % per, :, pl.ds(0, wide)] = q_t[r : r + 8, c : c + wide]

    def rs_copy(o):
        return pltpu.make_async_remote_copy(
            src_ref=q_parts.at[o],
            dst_ref=q_got.at[me],
            send_sem=rs_send.at[o],
            recv_sem=rs_recv.at[me],
            device_id={"ao": owner_dev[o]},
            device_id_type=MESH,
        )

    def ag_copy(o, dest):
        return pltpu.make_async_remote_copy(
            src_ref=q_sum,
            dst_ref=q_full.at[o],
            send_sem=ag_send.at[dest],
            recv_sem=ag_recv.at[o],
            device_id={"ao": dest},
            device_id_type=MESH,
        )

    for o in range(owners):
        @pl.when(me != owner_dev[o])
        def _():
            rs_copy(o).start()

    for o in range(owners):
        @pl.when(me == owner_dev[o])
        def _():
            q_sum[...] = q_parts[o]

            def add_step(d, carry):
                src = lax.rem(me + d, n)
                pltpu.make_async_remote_copy(
                    src_ref=q_parts.at[o],
                    dst_ref=q_got.at[src],
                    send_sem=rs_send.at[o],
                    recv_sem=rs_recv.at[src],
                    device_id={"ao": src},
                    device_id_type=MESH,
                ).wait_recv()
                q_sum[...] += q_got[src]
                return carry

            lax.fori_loop(1, n, add_step, 0)

            def spread_step(d, carry):
                ag_copy(o, lax.rem(me + d, n)).start()
                return carry

            lax.fori_loop(1, n, spread_step, 0)
            q_full[o] = q_sum[...]

    for o in range(owners):
        @pl.when(me != owner_dev[o])
        def _():
            ag_copy(o, owner_dev[o]).wait_recv()

    for k in range(blocks):
        r, c, wide = block_of(k)
        q_ref[pl.ds(r, 8), pl.ds(c, wide)] = q_full[k // per, k % per, :, pl.ds(0, wide)]

    def drain(d, carry):
        dest = lax.rem(me + d, n)
        slot_copy(dest, me).wait_send()
        return carry

    lax.fori_loop(1, n, drain, 0)
    for o in range(owners):
        @pl.when(me != owner_dev[o])
        def _():
            rs_copy(o).wait_send()

        @pl.when(me == owner_dev[o])
        def _():
            def done(d, carry):
                ag_copy(o, lax.rem(me + d, n)).wait_send()
                return carry

            lax.fori_loop(1, n, done, 0)


def hand_over(b_in, q_in, b_ref, q_ref):
    b_ref[...] = b_in[...]
    q_ref[...] = q_in[...]


def solution(mesh):
    n = mesh.shape["ao"]

    def on_device(chol_tiles, orbitals, rdm_two, tile_row, tile_col, tile_live):
        nao, norb = orbitals.shape
        vec_all = chol_tiles.shape[1]
        vec = vec_all // n
        rows = vec * ACT
        blocks = (ACT // 8) * (-(-norb // 128))
        per = -(-blocks // n)
        owners = -(-blocks // per)
        b, q_t = pl.pallas_call(
            functools.partial(kernel, n, vec, norb, per, owners),
            out_shape=(
                jax.ShapeDtypeStruct((rows, norb), BF16),
                jax.ShapeDtypeStruct((ACT, norb), F32),
            ),
            in_specs=[pl.BlockSpec(memory_space=pltpu.SMEM)] * 3
            + [pl.BlockSpec(memory_space=pl.ANY)] * 3,
            out_specs=(
                pl.BlockSpec(memory_space=pltpu.VMEM),
                pl.BlockSpec(memory_space=pltpu.VMEM),
            ),
            scratch_shapes=[
                pltpu.VMEM((vec_all, TILE, TILE), BF16),
                pltpu.VMEM((ACT_ROWS, nao), BF16),
                pltpu.VMEM((nao // TILE, ACT_ROWS, TILE), BF16),
                pltpu.VMEM((nao // TILE, norb, TILE), BF16),
                pltpu.VMEM(rdm_two.shape, BF16),
                pltpu.VMEM((n, rows, TILE), BF16),
                pltpu.VMEM((n, rows, TILE), BF16),
                pltpu.VMEM((rows, norb), F32),
                pltpu.VMEM((ACT, vec, ACT), F32),
                pltpu.VMEM((owners, per, 8, 128), F32),
                pltpu.VMEM((n, per, 8, 128), F32),
                pltpu.VMEM((per, 8, 128), F32),
                pltpu.VMEM((owners, per, 8, 128), F32),
                pltpu.SemaphoreType.DMA((4,)),
                pltpu.SemaphoreType.DMA((n,)),
                pltpu.SemaphoreType.DMA((n,)),
                pltpu.SemaphoreType.DMA((owners,)),
                pltpu.SemaphoreType.DMA((n,)),
                pltpu.SemaphoreType.DMA((n,)),
                pltpu.SemaphoreType.DMA((owners,)),
            ],
            compiler_params=pltpu.CompilerParams(
                collective_id=0, has_side_effects=True, vmem_limit_bytes=56 * 1024 * 1024
            ),
        )(
            tile_row, tile_col, tile_live, chol_tiles,
            orbitals.T, rdm_two,
        )
        b, q_t = pl.pallas_call(
            hand_over,
            out_shape=(
                jax.ShapeDtypeStruct((rows, norb), BF16),
                jax.ShapeDtypeStruct((ACT, norb), F32),
            ),
            in_specs=[pl.BlockSpec(memory_space=pltpu.VMEM)] * 2,
            out_specs=(pl.BlockSpec(memory_space=pltpu.VMEM),) * 2,
            compiler_params=pltpu.CompilerParams(vmem_limit_bytes=56 * 1024 * 1024),
        )(b, q_t)
        return b.reshape(vec, ACT, norb), q_t.T

    return jax.shard_map(
        on_device,
        mesh=mesh,
        in_specs=(
            P(("grp", "ao"), None, None, None),
            P("grp", None),
            P("grp", None),
            P("grp"),
            P("grp"),
            P("grp"),
        ),
        out_specs=(P(("grp", "ao"), None, None), P("grp", None)),
        check_vma=False,
    )
```

```python
import functools

import jax
import jax.numpy as jnp
from jax import lax
from jax.experimental import pallas as pl
from jax.experimental.pallas import tpu as pltpu
from jax.sharding import PartitionSpec as P

TILE = 128
ACT = 40
ACT_ROWS = 48
MESH = pl.DeviceIdType.MESH
F32 = jnp.float32
BF16 = jnp.bfloat16
NT_DIMS = (((1,), (1,)), ((), ()))


def kernel(
    n, vec, norb, per, owners,
    row_ref, col_ref, live_ref, chol_hbm, orb_hbm, rdm_hbm,
    b_ref, q_ref,
    chol, act_wide, act, orb, rdm, sent, got, acc, zeta_t, q_parts, q_got, q_sum, q_full,
    load_sem, send_sem, recv_sem, rs_send, rs_recv, ag_send, ag_recv,
):
    me = lax.axis_index("ao")
    rows = vec * ACT
    flat_len = ACT * ACT
    lane_blocks = -(-norb // 128)
    owner_dev = [(o * n) // owners for o in range(owners)]

    loads = [
        pltpu.make_async_copy(orb_hbm.at[pl.ds(0, ACT_ROWS)], act_wide, load_sem.at[0]),
        pltpu.make_async_copy(chol_hbm.at[0], chol, load_sem.at[1]),
        pltpu.make_async_copy(rdm_hbm, rdm, load_sem.at[2]),
    ]
    loads[0].start()
    loads[1].start()
    ntiles = orb.shape[0]

    barrier = pltpu.get_barrier_semaphore()

    def greet(d, carry):
        pl.semaphore_signal(
            barrier, inc=1, device_id={"ao": lax.rem(me + d, n)}, device_id_type=MESH
        )
        return carry

    lax.fori_loop(1, n, greet, 0)

    q_parts[...] = jnp.zeros_like(q_parts)
    live = live_ref[me].astype(F32)
    loads[0].wait()
    for k in range(ntiles):
        act[k] = act_wide[:, k * TILE : (k + 1) * TILE]
    cols_t = act[col_ref[me]]
    loads[1].wait()

    def half(dest):
        tiles = chol[pl.ds(dest * vec, vec)].reshape(vec * TILE, TILE)
        out = lax.dot_general(cols_t, tiles, NT_DIMS, preferred_element_type=F32)
        out = out[:ACT] * live
        parts = [out[:, v * TILE : (v + 1) * TILE] for v in range(vec)]
        return jnp.concatenate(parts, axis=0).astype(BF16)

    def distance(i):
        off = (i + 1) // 2
        return n // 2 + off * (2 * ((i + 1) % 2) - 1)

    def slot_copy(there, mine):
        return pltpu.make_async_remote_copy(
            src_ref=sent.at[there],
            dst_ref=got.at[mine],
            send_sem=send_sem.at[there],
            recv_sem=recv_sem.at[mine],
            device_id={"ao": there},
            device_id_type=MESH,
        )

    for k in range(ntiles):
        pltpu.make_async_copy(
            orb_hbm.at[:, pl.ds(k * TILE, TILE)], orb.at[k], load_sem.at[3]
        ).start()
    loads[2].start()

    def half_step(i, carry):
        dest = lax.rem(me + distance(i), n)
        sent[dest] = half(dest)
        return carry

    def send_step(i, carry):
        slot_copy(lax.rem(me + distance(i), n), me).start()
        return carry

    lax.fori_loop(0, n - 1, half_step, 0, unroll=n <= 16)
    pl.semaphore_wait(barrier, n - 1)
    lax.fori_loop(0, n - 1, send_step, 0, unroll=n <= 16)

    own = half(me)
    column = lax.broadcasted_iota(jnp.int32, (1, flat_len), 1)
    lane_of = column - (column // ACT) * ACT
    pick = (lax.broadcasted_iota(jnp.int32, (TILE, flat_len), 0) == lane_of).astype(F32).astype(BF16)
    mask = lax.broadcasted_iota(jnp.int32, (ACT, flat_len), 0) == column // ACT
    pltpu.make_async_copy(orb, orb, load_sem.at[3]).wait()

    def second(block, slot):
        return lax.dot_general(block, orb[row_ref[slot]], NT_DIMS, preferred_element_type=F32)

    acc[...] = second(own, me)

    def take_step(j, carry):
        src = lax.rem(me + n - distance(n - 2 - j), n)
        pltpu.make_async_remote_copy(
            src_ref=sent.at[src],
            dst_ref=got.at[src],
            send_sem=send_sem.at[src],
            recv_sem=recv_sem.at[src],
            device_id={"ao": src},
            device_id_type=MESH,
        ).wait_recv()
        acc[...] += second(got[src], src)
        return carry

    lax.fori_loop(0, n - 1, take_step, 0, unroll=n <= 16)

    b16 = acc[...].astype(BF16)
    b_ref[...] = b16
    spread = jnp.dot(b16[:, :TILE], pick, preferred_element_type=F32)
    flat = jnp.concatenate(
        [
            jnp.sum(jnp.where(mask, spread[v * ACT : (v + 1) * ACT], 0.0), axis=0, keepdims=True)
            for v in range(vec)
        ],
        axis=0,
    ).astype(BF16)
    loads[2].wait()
    zeta = jnp.dot(flat, rdm[...], preferred_element_type=F32)
    for t in range(ACT):
        zeta_t[t] = zeta[:, t * ACT : (t + 1) * ACT]
    b32 = b16.astype(F32)
    q_t = jnp.zeros((ACT, norb), F32)
    for v in range(vec):
        z = zeta_t[:, v, :]
        high = z.astype(BF16)
        low = (z - high.astype(F32)).astype(BF16)
        b_v = b32[v * ACT : (v + 1) * ACT].astype(BF16)
        q_t += jnp.dot(high, b_v, preferred_element_type=F32)
        q_t += jnp.dot(low, b_v, preferred_element_type=F32)

    def block_of(k):
        r, c = k // lane_blocks, k % lane_blocks
        return r * 8, c * 128, min(128, norb - c * 128)

    blocks = (ACT // 8) * lane_blocks
    for k in range(blocks):
        r, c, wide = block_of(k)
        q_parts[k // per, k % per, :, pl.ds(0, wide)] = q_t[r : r + 8, c : c + wide]

    def rs_copy(o):
        return pltpu.make_async_remote_copy(
            src_ref=q_parts.at[o],
            dst_ref=q_got.at[me],
            send_sem=rs_send.at[o],
            recv_sem=rs_recv.at[me],
            device_id={"ao": owner_dev[o]},
            device_id_type=MESH,
        )

    def ag_copy(o, dest):
        return pltpu.make_async_remote_copy(
            src_ref=q_sum,
            dst_ref=q_full.at[o],
            send_sem=ag_send.at[dest],
            recv_sem=ag_recv.at[o],
            device_id={"ao": dest},
            device_id_type=MESH,
        )

    for o in range(owners):
        @pl.when(me != owner_dev[o])
        def _():
            rs_copy(o).start()

    for o in range(owners):
        @pl.when(me == owner_dev[o])
        def _():
            q_sum[...] = q_parts[o]

            def add_step(d, carry):
                src = lax.rem(me + d, n)
                pltpu.make_async_remote_copy(
                    src_ref=q_parts.at[o],
                    dst_ref=q_got.at[src],
                    send_sem=rs_send.at[o],
                    recv_sem=rs_recv.at[src],
                    device_id={"ao": src},
                    device_id_type=MESH,
                ).wait_recv()
                q_sum[...] += q_got[src]
                return carry

            lax.fori_loop(1, n, add_step, 0)

            def spread_step(d, carry):
                ag_copy(o, lax.rem(me + d, n)).start()
                return carry

            lax.fori_loop(1, n, spread_step, 0)
            q_full[o] = q_sum[...]

    for o in range(owners):
        @pl.when(me != owner_dev[o])
        def _():
            ag_copy(o, owner_dev[o]).wait_recv()

    for k in range(blocks):
        r, c, wide = block_of(k)
        q_ref[pl.ds(r, 8), pl.ds(c, wide)] = q_full[k // per, k % per, :, pl.ds(0, wide)]

    def drain(d, carry):
        dest = lax.rem(me + d, n)
        slot_copy(dest, me).wait_send()
        return carry

    lax.fori_loop(1, n, drain, 0)
    for o in range(owners):
        @pl.when(me != owner_dev[o])
        def _():
            rs_copy(o).wait_send()

        @pl.when(me == owner_dev[o])
        def _():
            def done(d, carry):
                ag_copy(o, lax.rem(me + d, n)).wait_send()
                return carry

            lax.fori_loop(1, n, done, 0)


def hand_over(b_in, q_in, b_ref, q_ref):
    b_ref[...] = b_in[...]
    q_ref[...] = q_in[...]


def solution(mesh):
    n = mesh.shape["ao"]

    def on_device(chol_tiles, orbitals, rdm_two, tile_row, tile_col, tile_live):
        nao, norb = orbitals.shape
        vec_all = chol_tiles.shape[1]
        vec = vec_all // n
        rows = vec * ACT
        blocks = (ACT // 8) * (-(-norb // 128))
        per = -(-blocks // n)
        owners = -(-blocks // per)
        b, q_t = pl.pallas_call(
            functools.partial(kernel, n, vec, norb, per, owners),
            out_shape=(
                jax.ShapeDtypeStruct((rows, norb), BF16),
                jax.ShapeDtypeStruct((ACT, norb), F32),
            ),
            in_specs=[pl.BlockSpec(memory_space=pltpu.SMEM)] * 3
            + [pl.BlockSpec(memory_space=pl.ANY)] * 3,
            out_specs=(
                pl.BlockSpec(memory_space=pltpu.VMEM),
                pl.BlockSpec(memory_space=pltpu.VMEM),
            ),
            scratch_shapes=[
                pltpu.VMEM((vec_all, TILE, TILE), BF16),
                pltpu.VMEM((ACT_ROWS, nao), BF16),
                pltpu.VMEM((nao // TILE, ACT_ROWS, TILE), BF16),
                pltpu.VMEM((nao // TILE, norb, TILE), BF16),
                pltpu.VMEM(rdm_two.shape, BF16),
                pltpu.VMEM((n, rows, TILE), BF16),
                pltpu.VMEM((n, rows, TILE), BF16),
                pltpu.VMEM((rows, norb), F32),
                pltpu.VMEM((ACT, vec, ACT), F32),
                pltpu.VMEM((owners, per, 8, 128), F32),
                pltpu.VMEM((n, per, 8, 128), F32),
                pltpu.VMEM((per, 8, 128), F32),
                pltpu.VMEM((owners, per, 8, 128), F32),
                pltpu.SemaphoreType.DMA((4,)),
                pltpu.SemaphoreType.DMA((n,)),
                pltpu.SemaphoreType.DMA((n,)),
                pltpu.SemaphoreType.DMA((owners,)),
                pltpu.SemaphoreType.DMA((n,)),
                pltpu.SemaphoreType.DMA((n,)),
                pltpu.SemaphoreType.DMA((owners,)),
            ],
            compiler_params=pltpu.CompilerParams(
                collective_id=0, has_side_effects=True, vmem_limit_bytes=56 * 1024 * 1024
            ),
        )(
            tile_row, tile_col, tile_live, chol_tiles,
            orbitals.T, rdm_two,
        )
        b, q_t = pl.pallas_call(
            hand_over,
            out_shape=(
                jax.ShapeDtypeStruct((rows, norb), BF16),
                jax.ShapeDtypeStruct((ACT, norb), F32),
            ),
            in_specs=[pl.BlockSpec(memory_space=pltpu.VMEM)] * 2,
            out_specs=(pl.BlockSpec(memory_space=pltpu.VMEM),) * 2,
            compiler_params=pltpu.CompilerParams(vmem_limit_bytes=56 * 1024 * 1024),
        )(b, q_t)
        return b.reshape(vec, ACT, norb), q_t.T

    return jax.shard_map(
        on_device,
        mesh=mesh,
        in_specs=(
            P(("grp", "ao"), None, None, None),
            P("grp", None),
            P("grp", None),
            P("grp"),
            P("grp"),
            P("grp"),
        ),
        out_specs=(P(("grp", "ao"), None, None), P("grp", None)),
        check_vma=False,
    )
```
